256 devices in a mesh: row: 16 (over z, core), col: 16 (over y, x).
Axes of the slice: x: 4, y: 4, z: 8, core: 2. Of those that a mesh axis runs over, the one named last changes fastest.
Arguments:
- tokens: bfloat16 [1024, 12288], P('col', 'row'), may hold values from -6 to 6
- w_in: bfloat16 [12288, 24576], P('row', 'col'), may hold values from -0.0546875 to 0.0546875
- w_out: bfloat16 [24576, 12288], P('col', 'row'), may hold values from -0.0390625 to 0.0390625
- grad_out: bfloat16 [1024, 12288], P('col', 'row'), may hold values from -6 to 6
Outputs:
- layer_out: bfloat16 [1024, 12288], P('col', 'row')
- grad_tokens: bfloat16 [1024, 12288], P('col', 'row')
- grad_w_in: bfloat16 [12288, 24576], P('row', 'col')
- grad_w_out: bfloat16 [24576, 12288], P('col', 'row')
The draws below stay inside these ranges and needn't reach their ends.
All inputs are finite; a program needn't handle non-finite values.
Results may differ from the reference program's by a relative error of at most 0.0049.
Values may be sent and summed in bfloat16 or wider, within the bound.
A program may use at most 128 MiB of HBM per device.

```python
import jax
import jax.numpy as jnp
from jax import lax

D = 12288
FF = 24576
TOKENS = 1024


def level_of(rng, extent, cuts, low, largest):
    def one(position, shards_of):
        draws = jax.random.uniform(jax.random.fold_in(jax.random.fold_in(rng, 6), position), (shards_of,), jnp.float32, low / len(cuts), largest / len(cuts))
        return jnp.repeat(jnp.exp(draws), extent[position] // shards_of).reshape((-1,) + (1,) * (len(extent) - position - 1))

    level = one(*cuts[0])
    for cut in cuts[1:]:
        level = level * one(*cut)
    return level


def normal_values(stream_key, dims, scale, limit, split=(), kind=jnp.bfloat16):
    drawn = scale * jax.random.normal(stream_key, dims, jnp.float32)
    if split:
        drawn = drawn * level_of(stream_key, dims, split, -0.22, 0.18)
    return jnp.clip(drawn, -limit, limit).astype(kind)


def setup_inputs(seed: int = 0) -> dict:
    splits = jax.random.split(jax.random.key(seed), 5)
    return {
        "tokens": normal_values(splits[0], (TOKENS, D), 1.0, 6.0, ((0, 16), (1, 16))),
        "w_in": normal_values(splits[1], (D, FF), D ** -0.5, 0.0546875, ((0, 16), (1, 16))),
        "w_out": normal_values(splits[2], (FF, D), FF ** -0.5, 0.0390625, ((0, 16), (1, 16))),
        "grad_out": normal_values(splits[3], (TOKENS, D), 1.0, 6.0, ((0, 16), (1, 16))),
    }


gelu_coef = 0.7978845608


def gelu_tanh(values):
    tanh_arg = gelu_coef * (values + 0.044715 * values * values * values)
    return 0.5 * values * (1.0 + jnp.tanh(tanh_arg))


def gelu_slope(values):
    tanh_val = jnp.tanh(gelu_coef * (values + 0.044715 * values * values * values))
    return 0.5 * (1.0 + tanh_val) + 0.5 * values * (1.0 - tanh_val * tanh_val) * gelu_coef * (1.0 + 3.0 * 0.044715 * values * values)


def reference(tokens, w_in, w_out, grad_out):
    hidden = jnp.dot(tokens, w_in, preferred_element_type=jnp.float32)
    activation = gelu_tanh(hidden).astype(jnp.bfloat16)
    layer_out = jnp.dot(activation, w_out, preferred_element_type=jnp.float32).astype(jnp.bfloat16)
    grad_act = lax.dot_general(grad_out, w_out, (((1,), (1,)), ((), ())), preferred_element_type=jnp.float32)
    grad_hidden = (grad_act * gelu_slope(hidden)).astype(jnp.bfloat16)
    grad_w_out = lax.dot_general(activation, grad_out, (((0,), (0,)), ((), ())), preferred_element_type=jnp.float32).astype(jnp.bfloat16)
    grad_w_in = lax.dot_general(tokens, grad_hidden, (((0,), (0,)), ((), ())), preferred_element_type=jnp.float32).astype(jnp.bfloat16)
    grad_tokens = lax.dot_general(grad_hidden, w_in, (((1,), (1,)), ((), ())), preferred_element_type=jnp.float32).astype(jnp.bfloat16)
    return layer_out, grad_tokens, grad_w_in, grad_w_out
```

```python
import jax
import jax.numpy as jnp
from jax import lax
from jax.experimental import pallas as pl
from jax.experimental.pallas import tpu as pltpu
from jax.sharding import PartitionSpec as P

MESH = pl.DeviceIdType.MESH
BF = jnp.bfloat16
F32 = jnp.float32
gelu_coef = 0.7978845608

WAVES = 4
WROWS = 256
CH = 32
HALF = 768
TILE = 256


def wave_pieces():
    first = [(0, 0, 0, 64)]
    first += [(0, d, 0, 32) for d in (1, 3, 2)] + [(d, 0, 0, 32) for d in (1, 3, 2)]
    second = [(1, 3, 0, 64), (3, 1, 0, 64), (1, 1, 32, 32), (3, 3, 32, 32), (2, 2, 0, 64)]
    third = [(1, 2, 0, 64), (2, 1, 0, 64), (3, 2, 0, 64), (2, 3, 0, 64)]
    fourth = [(0, d, 32, 32) for d in (1, 3, 2)] + [(d, 0, 32, 32) for d in (1, 3, 2)]
    fourth += [(1, 1, 0, 32), (3, 3, 0, 32)]
    waves = []
    for pieces in (first, second, third, fourth):
        at, wave = 0, []
        for dy, dx, row0, rows in pieces:
            wave.append((dy, dx, row0, rows, at))
            at += rows
        waves.append(wave)
    return waves


PIECES = wave_pieces()
SENT_ROWS = [192, 256, 256, 256]


def gelu_and_slope(h):
    t = jnp.tanh(gelu_coef * (h + 0.044715 * h * h * h))
    act = 0.5 * h * (1.0 + t)
    slope = 0.5 * (1.0 + t) + 0.5 * h * (1.0 - t * t) * gelu_coef * (1.0 + 3.0 * 0.044715 * h * h)
    return act, slope


def dot_nn(a, b):
    return lax.dot_general(a, b, (((1,), (0,)), ((), ())), preferred_element_type=F32)


def dot_nt(a, b):
    return lax.dot_general(a, b, (((1,), (1,)), ((), ())), preferred_element_type=F32)


def dot_tn(a, b):
    return lax.dot_general(a, b, (((0,), (0,)), ((), ())), preferred_element_type=F32)


def kernel(
    tok_hbm, win_hbm, wout_hbm, gout_hbm,
    lo_hbm, gt_hbm, gwi_hbm, gwo_hbm,
    tg, w_in, w_out, pown, px, pr, sb, rb, ag, ob, outr, gwi, gwo, fin,
    loc_sem, a_ss, a_rs, px_ss, px_rs, rs_ss, rs_rs, ag_ss, ag_rs, x_ss, x_rs, o_ss, o_rs, out_sem,
):
    row, col = lax.axis_index("row"), lax.axis_index("col")
    z, c = row // 2, row % 2
    y, x = col // 4, col % 4
    sign = 1 - 2 * c

    def z_chip(d):
        return (z + d + 16) % 8

    fwd = (z_chip(sign) * 2 + c, col)
    back = (z_chip(-sign) * 2 + c, col)
    mate = (z * 2 + 1 - c, col)

    def plane(dy, dx):
        return (row, ((y + dy + 4) % 4) * 4 + (x + dx + 4) % 4)

    loads = [
        pltpu.make_async_copy(tok_hbm, tg.at[0, 0, pl.ds(0, 64)], loc_sem.at[0]),
        pltpu.make_async_copy(gout_hbm, tg.at[1, 0, pl.ds(0, 64)], loc_sem.at[1]),
        pltpu.make_async_copy(win_hbm, w_in, loc_sem.at[2]),
        pltpu.make_async_copy(wout_hbm, w_out, loc_sem.at[3]),
    ]
    for load in loads:
        load.start()

    barrier = pltpu.get_barrier_semaphore()
    greet = [fwd, back, mate] + [plane(d // 4, d % 4) for d in range(1, 16)]
    for dev in greet:
        pl.semaphore_signal(barrier, inc=1, device_id=dev, device_id_type=MESH)
    loads[0].wait()
    loads[1].wait()
    pl.semaphore_wait(barrier, len(greet))

    def remote(src, dst, ss, rs, dev):
        return pltpu.make_async_remote_copy(
            src_ref=src, dst_ref=dst, send_sem=ss, recv_sem=rs, device_id=dev, device_id_type=MESH
        )

    def wait_bytes(ref, sem):
        pltpu.make_async_copy(ref, ref, sem).wait()

    def push_a(w, arr):
        for dy, dx, row0, rows, at in PIECES[w]:
            if dy or dx:
                remote(
                    tg.at[arr, 0, pl.ds(row0, rows)],
                    tg.at[arr, w, pl.ds(at, rows)],
                    a_ss.at[arr, w],
                    a_rs.at[arr, w],
                    plane(-dy, -dx),
                ).start()

    def wait_a(w, arr):
        wait_bytes(tg.at[arr, w, pl.ds(WROWS - SENT_ROWS[w], SENT_ROWS[w])], a_rs.at[arr, w])

    def partial(w, op):
        def tile(start):
            if op == 0:
                return dot_nn(tg[0, w], w_in[:, pl.ds(start, TILE)])
            return dot_nt(tg[1, w], w_out[pl.ds(start, TILE), :])

        def theirs(j, carry):
            at = pl.multiple_of(j * TILE, TILE)
            px[w, op, :, pl.ds(at, TILE)] = tile(pl.multiple_of((1 - c) * HALF + at, TILE))
            return carry

        def mine(j, carry):
            at = pl.multiple_of(j * TILE, TILE)
            pown[w % 2, op, :, pl.ds(at, TILE)] = tile(pl.multiple_of(c * HALF + at, TILE))
            return carry

        lax.fori_loop(0, HALF // TILE, theirs, 0)
        remote(px.at[w, op], pr.at[w, op], px_ss.at[w, op], px_rs.at[w, op], mate).start()
        lax.fori_loop(0, HALF // TILE, mine, 0)

    def wait_px(w, op):
        wait_bytes(pr.at[w, op], px_rs.at[w, op])

    def own_term(w, op, k):
        rows = pl.ds(pl.multiple_of(k * CH, CH), CH)
        return pown[w % 2, op, rows, :] + pr[w, op, rows, :]

    def rs_send(w, op, n):
        k = z_chip(sign * (4 - n)) if n < 4 else z_chip(-sign * (7 - n))
        term = own_term(w, op, k)
        if n not in (0, 4):
            wait_bytes(rb.at[w, op, n - 1], rs_rs.at[w, op, n - 1])
            term = term + rb[w, op, n - 1].astype(F32)
        sb[w, op, n] = term.astype(BF)
        remote(
            sb.at[w, op, n], rb.at[w, op, n], rs_ss.at[w, op], rs_rs.at[w, op, n], fwd if n < 4 else back
        ).start()

    def rs_final(w, op):
        total = own_term(w, op, z)
        for n in (6, 3):
            wait_bytes(rb.at[w, op, n], rs_rs.at[w, op, n])
            total = total + rb[w, op, n].astype(F32)
        return total

    def ag_slot(w, op, k):
        return ag.at[op, w, c, pl.ds(pl.multiple_of(k * CH, CH), CH)]

    def finish_hidden(w):
        hidden = rs_final(w, 0)
        act, slope = gelu_and_slope(hidden)
        rows = pl.ds(pl.multiple_of(z * CH, CH), CH)
        ag[0, w, c, rows, :] = act.astype(BF)
        ag[1, w, c, rows, :] = (rs_final(w, 1) * slope).astype(BF)

    def ag_wait(w, op, n):
        wait_bytes(sb.at[w, op, n], ag_rs.at[w, op, n])

    def ag_send(w, op, n):
        k = z_chip(-sign * n) if n < 4 else z_chip(sign * (n - 4))
        if n not in (0, 4):
            ag_wait(w, op, n - 1)
        slot = ag_slot(w, op, k)
        remote(slot, slot, ag_ss.at[w, op], ag_rs.at[w, op, n], fwd if n < 4 else back).start()

    def x_send(w, op):
        ag_wait(w, op, 6)
        ag_wait(w, op, 3)
        half = ag.at[op, w, c]
        remote(half, half, x_ss.at[w, op], x_rs.at[w, op], mate).start()

    def x_wait(w, op):
        wait_bytes(ag.at[op, w, 1 - c], x_rs.at[w, op])

    def outputs(w, op):
        def tile(j, carry):
            at = pl.ds(pl.multiple_of(j * TILE, TILE), TILE)
            if op == 0:
                total = dot_nn(ag[0, w, 0], w_out[pl.ds(0, HALF), at])
                total += dot_nn(ag[0, w, 1], w_out[pl.ds(HALF, HALF), at])
            else:
                total = dot_nt(ag[1, w, 0], w_in[at, pl.ds(0, HALF)])
                total += dot_nt(ag[1, w, 1], w_in[at, pl.ds(HALF, HALF)])
            ob[w, op, :, at] = total.astype(BF)
            return carry

        lax.fori_loop(0, HALF // TILE, tile, 0)
        for dy, dx, row0, rows, at in PIECES[w]:
            if dy or dx:
                remote(
                    ob.at[w, op, pl.ds(at, rows)],
                    outr.at[op, dy * 4 + dx, pl.ds(row0, rows)],
                    o_ss.at[w, op],
                    o_rs.at[w, op],
                    plane(dy, dx),
                ).start()

    def phase(p):
        rs, gather = p < WAVES, p >= 1
        for s in range(4):
            for op in range(2):
                if rs:
                    if s == 0:
                        wait_px(p, op)
                    rs_send(p, op, s)
                    if s < 3:
                        rs_send(p, op, 4 + s)
            if gather:
                for op in range(2):
                    ag_send(p - 1, op, s)
                    if s < 3:
                        ag_send(p - 1, op, 4 + s)
            if s == 0 and p + 1 < WAVES:
                wait_a(p + 1, 0)
                wait_a(p + 1, 1)
                if p + 2 < WAVES:
                    push_a(p + 2, 0)
                    push_a(p + 2, 1)
                partial(p + 1, 0)
            if s == 1 and p + 1 < WAVES:
                partial(p + 1, 1)
            if s >= 2 and p >= 2:
                x_wait(p - 2, s - 2)
                outputs(p - 2, s - 2)
        if rs:
            finish_hidden(p)
        if gather:
            x_send(p - 1, 0)
            x_send(p - 1, 1)

    push_a(0, 0)
    push_a(0, 1)
    loads[2].wait()
    loads[3].wait()
    wait_a(0, 0)
    push_a(1, 0)
    partial(0, 0)
    wait_a(0, 1)
    push_a(1, 1)
    partial(0, 1)
    for p in range(WAVES + 1):
        phase(p)
    last = WAVES - 1
    for op in range(2):
        x_wait(last, op)
        outputs(last, op)

    def grad_w_out(i, carry):
        hf, j = i // 3, i % 3
        units = pl.ds(pl.multiple_of(j * TILE, TILE), TILE)
        total = dot_tn(ag[0, 0, hf, :, units], tg[1, 0])
        for w in range(1, WAVES):
            total += dot_tn(ag[0, w, hf, :, units], tg[1, w])
        rows = pl.ds(pl.multiple_of(i * TILE, TILE), TILE)
        gwo[rows, :] = total.astype(BF)
        return carry

    def grad_w_in(i, carry):
        hf, j = i // 3, i % 3
        units = pl.ds(pl.multiple_of(j * TILE, TILE), TILE)
        total = dot_tn(tg[0, 0, :, units], ag[1, 0, hf])
        for w in range(1, WAVES):
            total += dot_tn(tg[0, w, :, units], ag[1, w, hf])
        gwi[units, pl.ds(pl.multiple_of(hf * HALF, HALF), HALF)] = total.astype(BF)
        return carry

    lax.fori_loop(0, 6, grad_w_out, 0)
    put_gwo = pltpu.make_async_copy(gwo, gwo_hbm, out_sem.at[0])
    put_gwo.start()
    lax.fori_loop(0, 6, grad_w_in, 0)
    put_gwi = pltpu.make_async_copy(gwi, gwi_hbm, out_sem.at[1])
    put_gwi.start()

    puts = [put_gwo, put_gwi]
    for op, out in ((0, lo_hbm), (1, gt_hbm)):
        for w in range(WAVES):
            wait_bytes(ob.at[w, op, pl.ds(WROWS - SENT_ROWS[w], SENT_ROWS[w])], o_rs.at[w, op])

        def add_up(i, carry, op=op):
            rows = pl.ds(pl.multiple_of(i * 16, 16), 16)
            total = ob[0, op, rows, :].astype(F32)
            for slot in range(1, 16):
                total = total + outr[op, slot, rows, :].astype(F32)
            fin[op, rows, :] = total.astype(BF)
            return carry

        lax.fori_loop(0, 4, add_up, 0)
        put = pltpu.make_async_copy(fin.at[op], out, out_sem.at[2 + op])
        put.start()
        puts.append(put)

    for w in range(WAVES):
        sent = pl.ds(WROWS - SENT_ROWS[w], SENT_ROWS[w])
        for op in range(2):
            wait_bytes(tg.at[op, w, sent], a_ss.at[op, w])
            wait_bytes(px.at[w, op], px_ss.at[w, op])
            wait_bytes(sb.at[w, op], rs_ss.at[w, op])
            wait_bytes(sb.at[w, op], ag_ss.at[w, op])
            wait_bytes(ag.at[op, w, c], x_ss.at[w, op])
            wait_bytes(ob.at[w, op, sent], o_ss.at[w, op])
    for put in puts:
        put.wait()


def body(tokens, w_in, w_out, grad_out):
    dma = pltpu.SemaphoreType.DMA
    any_spec = pl.BlockSpec(memory_space=pl.ANY)
    return pl.pallas_call(
        kernel,
        name="ffn",
        out_shape=(
            jax.ShapeDtypeStruct((64, HALF), BF),
            jax.ShapeDtypeStruct((64, HALF), BF),
            jax.ShapeDtypeStruct((HALF, 2 * HALF), BF),
            jax.ShapeDtypeStruct((2 * HALF, HALF), BF),
        ),
        in_specs=[any_spec] * 4,
        out_specs=[any_spec] * 4,
        scratch_shapes=[
            pltpu.VMEM((2, WAVES, WROWS, HALF), BF),
            pltpu.VMEM((HALF, 2 * HALF), BF),
            pltpu.VMEM((2 * HALF, HALF), BF),
            pltpu.VMEM((2, 2, WROWS, HALF), F32),
            pltpu.VMEM((WAVES, 2, WROWS, HALF), F32),
            pltpu.VMEM((WAVES, 2, WROWS, HALF), F32),
            pltpu.VMEM((WAVES, 2, 7, CH, HALF), BF),
            pltpu.VMEM((WAVES, 2, 7, CH, HALF), BF),
            pltpu.VMEM((2, WAVES, 2, WROWS, HALF), BF),
            pltpu.VMEM((WAVES, 2, WROWS, HALF), BF),
            pltpu.VMEM((2, 16, 64, HALF), BF),
            pltpu.VMEM((HALF, 2 * HALF), BF),
            pltpu.VMEM((2 * HALF, HALF), BF),
            pltpu.VMEM((2, 64, HALF), BF),
            dma((4,)),
            dma((2, WAVES)), dma((2, WAVES)),
            dma((WAVES, 2)), dma((WAVES, 2)),
            dma((WAVES, 2)), dma((WAVES, 2, 7)),
            dma((WAVES, 2)), dma((WAVES, 2, 7)),
            dma((WAVES, 2)), dma((WAVES, 2)),
            dma((WAVES, 2)), dma((WAVES, 2)),
            dma((4,)),
        ],
        compiler_params=pltpu.CompilerParams(
            collective_id=0, has_side_effects=True, vmem_limit_bytes=60 << 20
        ),
        cost_estimate=pl.CostEstimate(flops=14500000000, bytes_accessed=10000000, transcendentals=2000000),
    )(tokens, w_in, w_out, grad_out)


def solution(mesh):
    placed = (P("col", "row"), P("row", "col"), P("col", "row"), P("col", "row"))
    return jax.shard_map(
        body,
        mesh=mesh,
        in_specs=placed,
        out_specs=(P("col", "row"), P("col", "row"), P("row", "col"), P("col", "row")),
        check_vma=False,
    )
```

```python
import jax
import jax.numpy as jnp
from jax import lax
from jax.experimental import pallas as pl
from jax.experimental.pallas import tpu as pltpu
from jax.sharding import PartitionSpec as P

MESH = pl.DeviceIdType.MESH
BF = jnp.bfloat16
F32 = jnp.float32
gelu_coef = 0.7978845608

WAVES = 4
ROWS = 256
PART = 16
START = [0, 2, 4, 6]
CH = 32
HALF = 768
TILE = 256


def part_of(dy, dx):
    if dy == 0:
        return PART * dx
    if dx == 0:
        return PART * (3 + dy)
    return PART * (7 + 3 * (dy - 1) + dx - 1)


def gelu_and_slope(h):
    t = jnp.tanh(gelu_coef * (h + 0.044715 * h * h * h))
    act = 0.5 * h * (1.0 + t)
    slope = 0.5 * (1.0 + t) + 0.5 * h * (1.0 - t * t) * gelu_coef * (1.0 + 3.0 * 0.044715 * h * h)
    return act, slope


def dot_nn(a, b):
    return lax.dot_general(a, b, (((1,), (0,)), ((), ())), preferred_element_type=F32)


def dot_nt(a, b):
    return lax.dot_general(a, b, (((1,), (1,)), ((), ())), preferred_element_type=F32)


def dot_tn(a, b):
    return lax.dot_general(a, b, (((0,), (0,)), ((), ())), preferred_element_type=F32)


def kernel(
    tok_hbm, win_hbm, wout_hbm, gout_hbm,
    lo, gt, gwi, gwo,
    shard, tg, w_in, w_out, pown, px, pr, sb, rb, ag, ob, outr,
    loc_sem, a_ss, a_rs, r_ss, r_rs, px_ss, px_rs, rs_ss, rs_rs, ag_ss, ag_rs, x_ss, x_rs, o_ss, o_rs,
):
    row, col = lax.axis_index("row"), lax.axis_index("col")
    z, c = row // 2, row % 2
    y, x = col // 4, col % 4
    sign = 1 - 2 * c

    def z_chip(d):
        return (z + d + 16) % 8

    fwd = (z_chip(sign) * 2 + c, col)
    back = (z_chip(-sign) * 2 + c, col)
    mate = (z * 2 + 1 - c, col)

    def plane(dy, dx):
        return (row, ((y + dy + 4) % 4) * 4 + (x + dx + 4) % 4)

    shards = [
        pltpu.make_async_copy(tok_hbm, shard.at[0], loc_sem.at[0]),
        pltpu.make_async_copy(gout_hbm, shard.at[1], loc_sem.at[1]),
    ]
    loads = [
        pltpu.make_async_copy(win_hbm, w_in, loc_sem.at[2]),
        pltpu.make_async_copy(wout_hbm, w_out, loc_sem.at[3]),
    ]
    for load in shards + loads:
        load.start()

    barrier = pltpu.get_barrier_semaphore()
    greet = [fwd, back, mate] + [plane(d // 4, d % 4) for d in range(1, 16)]
    for dev in greet:
        pl.semaphore_signal(barrier, inc=1, device_id=dev, device_id_type=MESH)
    for load in shards:
        load.wait()
    for arr in range(2):
        for w in range(WAVES):
            tg[arr, pl.ds(ROWS * w, PART), :] = shard[arr, pl.ds(PART * w, PART), :]
    pl.semaphore_wait(barrier, len(greet))

    def remote(src, dst, ss, rs, dev):
        return pltpu.make_async_remote_copy(
            src_ref=src, dst_ref=dst, send_sem=ss, recv_sem=rs, device_id=dev, device_id_type=MESH
        )

    def wait_bytes(ref, sem):
        pltpu.make_async_copy(ref, ref, sem).wait()

    def push_cross(w, arr):
        for dy, dx in ((0, 1), (1, 0), (0, 3), (3, 0), (0, 2), (2, 0)):
            remote(
                shard.at[arr, pl.ds(PART * w, PART)],
                tg.at[arr, pl.ds(ROWS * w + part_of(dy, dx), PART)],
                a_ss.at[arr, w],
                a_rs.at[arr, w],
                plane(-dy, -dx),
            ).start()

    def cross_rows(w, arr):
        return tg.at[arr, pl.ds(ROWS * w + PART, 6 * PART)]

    def wait_cross(w, arr):
        wait_bytes(cross_rows(w, arr), a_rs.at[arr, w])

    def push_relay(w, arr):
        def send(src, dst, rows, dev):
            remote(
                tg.at[arr, pl.ds(ROWS * w + src, rows)],
                tg.at[arr, pl.ds(ROWS * w + dst, rows)],
                r_ss.at[arr, w],
                r_rs.at[arr, w],
                dev,
            ).start()

        for d in (1, 3):
            send(part_of(0, 1), part_of(d, 1), 3 * PART, plane(-d, 0))
            send(part_of(2, 0), part_of(2, d), PART, plane(0, -d))
        send(part_of(2, 0), part_of(2, 2), PART, plane(0, -2))

    def relay_rows(w, arr):
        return tg.at[arr, pl.ds(ROWS * w + 7 * PART, 9 * PART)]

    def wait_relay(w, arr):
        wait_bytes(relay_rows(w, arr), r_rs.at[arr, w])

    def forward(w):
        for arr in range(2):
            wait_cross(w, arr)
            push_relay(w, arr)

    def product(w, op, start):
        tokens = tg[op, pl.ds(ROWS * w, ROWS), :]
        if op == 0:
            return dot_nn(tokens, w_in[:, pl.ds(start, TILE)])
        return dot_nt(tokens, w_out[pl.ds(start, TILE), :])

    def px_ref(w, op):
        return px.at[w % 2, op]

    def theirs(w, op):
        if w >= 2:
            wait_bytes(px_ref(w - 2, op), px_ss.at[w - 2, op])

        def tile(j, carry):
            at = pl.multiple_of(j * TILE, TILE)
            px[w % 2, op, :, pl.ds(at, TILE)] = product(
                w, op, pl.multiple_of((1 - c) * HALF + at, TILE)
            )
            return carry

        lax.fori_loop(0, HALF // TILE, tile, 0)
        remote(
            px_ref(w, op), pr.at[op, pl.ds(ROWS * w, ROWS)], px_ss.at[w, op], px_rs.at[w, op], mate
        ).start()

    def mine(w, op):
        def tile(j, carry):
            at = pl.multiple_of(j * TILE, TILE)
            pown[op, pl.ds(ROWS * w, ROWS), pl.ds(at, TILE)] = product(
                w, op, pl.multiple_of(c * HALF + at, TILE)
            )
            return carry

        lax.fori_loop(0, HALF // TILE, tile, 0)

    def wait_px(w, op):
        wait_bytes(pr.at[op, pl.ds(ROWS * w, ROWS)], px_rs.at[w, op])

    def own_term(w, op, k):
        at = pl.multiple_of(k * CH, CH)
        return pown[op, pl.ds(ROWS * w + at, CH), :] + pr[op, pl.ds(ROWS * w + at, CH), :]

    def slot(w, n):
        return pl.ds((7 * w + n) * CH, CH)

    def rs_send(w, op, n):
        k = z_chip(sign * (4 - n)) if n < 4 else z_chip(-sign * (7 - n))
        term = own_term(w, op, k)
        if n not in (0, 4):
            wait_bytes(rb.at[op, slot(w, n - 1)], rs_rs.at[w, op, n - 1])
            term = term + rb[op, slot(w, n - 1), :].astype(F32)
        sb[op, slot(w, n), :] = term.astype(BF)
        remote(
            sb.at[op, slot(w, n)], rb.at[op, slot(w, n)], rs_ss.at[w, op], rs_rs.at[w, op, n],
            fwd if n < 4 else back,
        ).start()

    def rs_final(w, op):
        total = own_term(w, op, z)
        for n in (6, 3):
            wait_bytes(rb.at[op, slot(w, n)], rs_rs.at[w, op, n])
            total = total + rb[op, slot(w, n), :].astype(F32)
        return total

    def chunk(w, k):
        return pl.ds(ROWS * w + pl.multiple_of(k * CH, CH), CH)

    def finish_hidden(w):
        hidden = rs_final(w, 0)
        act, slope = gelu_and_slope(hidden)
        ag[0, c, chunk(w, z), :] = act.astype(BF)
        ag[1, c, chunk(w, z), :] = (rs_final(w, 1) * slope).astype(BF)

    def ag_wait(w, op, n):
        wait_bytes(sb.at[op, slot(w, n)], ag_rs.at[w, op, n])

    def ag_send(w, op, n):
        k = z_chip(-sign * n) if n < 4 else z_chip(sign * (n - 4))
        if n not in (0, 4):
            ag_wait(w, op, n - 1)
        part = ag.at[op, c, chunk(w, k)]
        remote(part, part, ag_ss.at[w, op], ag_rs.at[w, op, n], fwd if n < 4 else back).start()

    def half_ref(w, op, half):
        return ag.at[op, half, pl.ds(ROWS * w, ROWS)]

    def x_send(w, op):
        ag_wait(w, op, 6)
        ag_wait(w, op, 3)
        remote(half_ref(w, op, c), half_ref(w, op, c), x_ss.at[w, op], x_rs.at[w, op], mate).start()

    def x_wait(w, op):
        wait_bytes(half_ref(w, op, 1 - c), x_rs.at[w, op])

    def outputs(w, op):
        tokens = pl.ds(ROWS * w, ROWS)

        def tile(j, carry):
            at = pl.ds(pl.multiple_of(j * TILE, TILE), TILE)
            if op == 0:
                total = dot_nn(ag[0, 0, tokens, :], w_out[pl.ds(0, HALF), at])
                total += dot_nn(ag[0, 1, tokens, :], w_out[pl.ds(HALF, HALF), at])
            else:
                total = dot_nt(ag[1, 0, tokens, :], w_in[at, pl.ds(0, HALF)])
                total += dot_nt(ag[1, 1, tokens, :], w_in[at, pl.ds(HALF, HALF)])
            ob[op, tokens, at] = total.astype(BF)
            return carry

        lax.fori_loop(0, HALF // TILE, tile, 0)
        for n in (4, 1, 12, 3, 8, 2, 5, 15, 7, 13, 6, 9, 14, 11, 10):
            dy, dx = n // 4, n % 4
            remote(
                ob.at[op, pl.ds(ROWS * w + part_of(dy, dx), PART)],
                outr.at[op, n, pl.ds(PART * w, PART)],
                o_ss.at[w, op],
                o_rs.at[w, op],
                plane(dy, dx),
            ).start()

    def o_rows(w, op):
        return ob.at[op, pl.ds(ROWS * w + PART, ROWS - PART)]

    def weight_grad(which, hf):
        def tile(j, carry):
            units = pl.ds(pl.multiple_of(j * TILE, TILE), TILE)
            if which == 0:
                total = dot_tn(ag[0, hf, :, units], tg[1])
                gwo[pl.ds(pl.multiple_of(hf * HALF + j * TILE, TILE), TILE), :] = total.astype(BF)
            else:
                total = dot_tn(tg[0, :, units], ag[1, hf])
                gwi[units, pl.ds(pl.multiple_of(hf * HALF, HALF), HALF)] = total.astype(BF)
            return carry

        lax.fori_loop(0, 3, tile, 0)

    def tick(t):
        ages = [t - START[w] for w in range(WAVES)]
        for w in range(WAVES):
            age = ages[w]
            if 1 <= age <= 3:
                for op in range(2):
                    rs_send(w, op, age)
                    if age < 3:
                        rs_send(w, op, 4 + age)
            if age == 4:
                finish_hidden(w)
            if 4 <= age <= 7:
                for op in range(2):
                    ag_send(w, op, age - 4)
                    if age > 4:
                        ag_send(w, op, age - 1)
            if age == 8:
                x_send(w, 0)
                x_send(w, 1)
        for w in range(WAVES):
            if ages[w] == 0:
                for op in range(2):
                    wait_px(w, op)
                    rs_send(w, op, 0)
                    rs_send(w, op, 4)
        if t in (1, 2):
            forward(t + 1)
        for w in range(1, WAVES):
            if ages[w] == -1:
                for op in range(2):
                    wait_relay(w, op)
                    theirs(w, op)
                mine(w, 0)
                mine(w, 1)
        for w in range(WAVES - 1):
            if ages[w] == 9:
                for op in range(2):
                    x_wait(w, op)
                    outputs(w, op)

    push_cross(0, 0)
    push_cross(0, 1)
    forward(0)
    push_cross(1, 0)
    push_cross(1, 1)
    for load in loads:
        load.wait()
    for op in range(2):
        wait_relay(0, op)
        theirs(0, op)
    forward(1)
    for w in (2, 3):
        push_cross(w, 0)
        push_cross(w, 1)
    mine(0, 0)
    mine(0, 1)
    for t in range(START[-1] + 9):
        tick(t)
    last = WAVES - 1
    weight_grad(0, c)
    for op in range(2):
        x_wait(last, op)
        outputs(last, op)
    weight_grad(0, 1 - c)
    weight_grad(1, c)
    weight_grad(1, 1 - c)

    def add_up(w, carry):
        mine_at = pl.multiple_of(w * ROWS, ROWS)
        at = pl.ds(pl.multiple_of(w * PART, PART), PART)
        for op, out in ((0, lo), (1, gt)):
            total = ob[op, pl.ds(mine_at, PART), :].astype(F32)
            for n in range(1, 16):
                total = total + outr[op, n, at, :].astype(F32)
            out[at, :] = total.astype(BF)
        return carry

    for w in range(last):
        for op in range(2):
            wait_bytes(o_rows(w, op), o_rs.at[w, op])
    lax.fori_loop(0, last, add_up, 0)
    for op in range(2):
        wait_bytes(o_rows(last, op), o_rs.at[last, op])
    lax.fori_loop(last, WAVES, add_up, 0)

    for w in range(WAVES):
        messages = pl.ds(7 * w * CH, 7 * CH)
        for op in range(2):
            wait_bytes(cross_rows(w, op), a_ss.at[op, w])
            wait_bytes(relay_rows(w, op), r_ss.at[op, w])
            if w >= WAVES - 2:
                wait_bytes(px_ref(w, op), px_ss.at[w, op])
            wait_bytes(sb.at[op, messages], rs_ss.at[w, op])
            wait_bytes(sb.at[op, messages], ag_ss.at[w, op])
            wait_bytes(half_ref(w, op, c), x_ss.at[w, op])
            wait_bytes(o_rows(w, op), o_ss.at[w, op])


OUT_SHAPES = ((64, HALF), (64, HALF), (HALF, 2 * HALF), (2 * HALF, HALF))


def write_out(*refs):
    sems = refs[8]
    copies = []
    for i, rows in ((2, 96), (3, 192), (0, 64), (1, 64)):
        for at in range(0, OUT_SHAPES[i][0], rows):
            part = pl.ds(at, rows)
            copies.append(pltpu.make_async_copy(refs[i].at[part], refs[4 + i].at[part], sems.at[len(copies)]))
    for copy in copies:
        copy.start()
    for copy in copies:
        copy.wait()


def body(tokens, w_in, w_out, grad_out):
    dma = pltpu.SemaphoreType.DMA
    any_spec = pl.BlockSpec(memory_space=pl.ANY)
    results = pl.pallas_call(
        kernel,
        name="ffn",
        out_shape=tuple(pltpu.VMEM(shape, BF) for shape in OUT_SHAPES),
        in_specs=[any_spec] * 4,
        out_specs=[pl.BlockSpec(memory_space=pltpu.VMEM)] * 4,
        scratch_shapes=[
            pltpu.VMEM((2, 64, HALF), BF),
            pltpu.VMEM((2, 1024, HALF), BF),
            pltpu.VMEM((HALF, 2 * HALF), BF),
            pltpu.VMEM((2 * HALF, HALF), BF),
            pltpu.VMEM((2, 1024, HALF), F32),
            pltpu.VMEM((2, 2, 256, HALF), F32),
            pltpu.VMEM((2, 1024, HALF), F32),
            pltpu.VMEM((2, 7 * 128, HALF), BF),
            pltpu.VMEM((2, 7 * 128, HALF), BF),
            pltpu.VMEM((2, 2, 1024, HALF), BF),
            pltpu.VMEM((2, 1024, HALF), BF),
            pltpu.VMEM((2, 16, 64, HALF), BF),
            dma((4,)),
            dma((2, WAVES)), dma((2, WAVES)),
            dma((2, WAVES)), dma((2, WAVES)),
            dma((WAVES, 2)), dma((WAVES, 2)),
            dma((WAVES, 2)), dma((WAVES, 2, 7)),
            dma((WAVES, 2)), dma((WAVES, 2, 7)),
            dma((WAVES, 2)), dma((WAVES, 2)),
            dma((WAVES, 2)), dma((WAVES, 2)),
        ],
        compiler_params=pltpu.CompilerParams(
            collective_id=0, has_side_effects=True, vmem_limit_bytes=50 << 20
        ),
        cost_estimate=pl.CostEstimate(flops=14500000000, bytes_accessed=10000000, transcendentals=2000000),
    )(tokens, w_in, w_out, grad_out)
    return pl.pallas_call(
        write_out,
        name="write_out",
        out_shape=tuple(jax.ShapeDtypeStruct(shape, BF) for shape in OUT_SHAPES),
        in_specs=[any_spec] * 4,
        out_specs=[any_spec] * 4,
        compiler_params=pltpu.CompilerParams(vmem_limit_bytes=1 << 20),
        scratch_shapes=[dma((18,))],
        cost_estimate=pl.CostEstimate(flops=0, bytes_accessed=10000000, transcendentals=0),
    )(*[pltpu.with_memory_space_constraint(r, pltpu.VMEM) for r in results])


def solution(mesh):
    placed = (P("col", "row"), P("row", "col"), P("col", "row"), P("col", "row"))
    return jax.shard_map(
        body,
        mesh=mesh,
        in_specs=placed,
        out_specs=(P("col", "row"), P("col", "row"), P("row", "col"), P("col", "row")),
        check_vma=False,
    )
```

```python
import jax
import jax.numpy as jnp
from jax import lax
from jax.experimental import pallas as pl
from jax.experimental.pallas import tpu as pltpu
from jax.sharding import PartitionSpec as P

MESH = pl.DeviceIdType.MESH
BF = jnp.bfloat16
F32 = jnp.float32
gelu_coef = 0.7978845608

WAVES = 4
ROWS = 256
PART = 16
START = [0, 2, 4, 6]
CH = 32
HALF = 768
TILE = 256


def part_of(dy, dx):
    if dy == 0:
        return PART * dx
    if dx == 0:
        return PART * (3 + dy)
    return PART * (7 + 3 * (dy - 1) + dx - 1)


def gelu_and_slope(h):
    t = jnp.tanh(gelu_coef * (h + 0.044715 * h * h * h))
    act = 0.5 * h * (1.0 + t)
    slope = 0.5 * (1.0 + t) + 0.5 * h * (1.0 - t * t) * gelu_coef * (1.0 + 3.0 * 0.044715 * h * h)
    return act, slope


def dot_nn(a, b):
    return lax.dot_general(a, b, (((1,), (0,)), ((), ())), preferred_element_type=F32)


def dot_nt(a, b):
    return lax.dot_general(a, b, (((1,), (1,)), ((), ())), preferred_element_type=F32)


def dot_tn(a, b):
    return lax.dot_general(a, b, (((0,), (0,)), ((), ())), preferred_element_type=F32)


def kernel(
    tok_hbm, win_hbm, wout_hbm, gout_hbm,
    lo, gt, gwi, gwo,
    shard, tg, w_in, w_out, pown, px, pr, sb, rb, ag, ob, outr,
    loc_sem, a_ss, a_rs, r_ss, r_rs, px_ss, px_rs, rs_ss, rs_rs, ag_ss, ag_rs, x_ss, x_rs, o_ss, o_rs,
):
    row, col = lax.axis_index("row"), lax.axis_index("col")
    z, c = row // 2, row % 2
    y, x = col // 4, col % 4
    sign = 1 - 2 * c

    def z_chip(d):
        return (z + d + 16) % 8

    fwd = (z_chip(sign) * 2 + c, col)
    back = (z_chip(-sign) * 2 + c, col)
    mate = (z * 2 + 1 - c, col)

    def plane(dy, dx):
        return (row, ((y + dy + 4) % 4) * 4 + (x + dx + 4) % 4)

    shards = [
        pltpu.make_async_copy(tok_hbm, shard.at[0], loc_sem.at[0]),
        pltpu.make_async_copy(gout_hbm, shard.at[1], loc_sem.at[1]),
    ]
    loads = [
        pltpu.make_async_copy(win_hbm, w_in, loc_sem.at[2]),
        pltpu.make_async_copy(wout_hbm, w_out, loc_sem.at[3]),
    ]
    for load in shards + loads:
        load.start()

    barrier = pltpu.get_barrier_semaphore()
    greet = [fwd, back, mate] + [plane(d // 4, d % 4) for d in range(1, 16)]
    for dev in greet:
        pl.semaphore_signal(barrier, inc=1, device_id=dev, device_id_type=MESH)
    for load in shards:
        load.wait()
    for arr in range(2):
        for w in range(WAVES):
            tg[arr, pl.ds(ROWS * w, PART), :] = shard[arr, pl.ds(PART * w, PART), :]
    pl.semaphore_wait(barrier, len(greet))

    def remote(src, dst, ss, rs, dev):
        return pltpu.make_async_remote_copy(
            src_ref=src, dst_ref=dst, send_sem=ss, recv_sem=rs, device_id=dev, device_id_type=MESH
        )

    def wait_bytes(ref, sem):
        pltpu.make_async_copy(ref, ref, sem).wait()

    def push_cross(w, arr):
        for dy, dx in ((0, 1), (1, 0), (0, 3), (3, 0), (0, 2), (2, 0)):
            remote(
                shard.at[arr, pl.ds(PART * w, PART)],
                tg.at[arr, pl.ds(ROWS * w + part_of(dy, dx), PART)],
                a_ss.at[arr, w],
                a_rs.at[arr, w],
                plane(-dy, -dx),
            ).start()

    def cross_rows(w, arr):
        return tg.at[arr, pl.ds(ROWS * w + PART, 6 * PART)]

    def wait_cross(w, arr):
        wait_bytes(cross_rows(w, arr), a_rs.at[arr, w])

    def push_relay(w, arr):
        def send(src, dst, rows, dev):
            remote(
                tg.at[arr, pl.ds(ROWS * w + src, rows)],
                tg.at[arr, pl.ds(ROWS * w + dst, rows)],
                r_ss.at[arr, w],
                r_rs.at[arr, w],
                dev,
            ).start()

        for d in (1, 3):
            send(part_of(0, 1), part_of(d, 1), 3 * PART, plane(-d, 0))
            send(part_of(2, 0), part_of(2, d), PART, plane(0, -d))
        send(part_of(2, 0), part_of(2, 2), PART, plane(0, -2))

    def relay_rows(w, arr):
        return tg.at[arr, pl.ds(ROWS * w + 7 * PART, 9 * PART)]

    def wait_relay(w, arr):
        wait_bytes(relay_rows(w, arr), r_rs.at[arr, w])

    def forward(w):
        for arr in range(2):
            wait_cross(w, arr)
            push_relay(w, arr)

    def product(w, op, start):
        tokens = tg[op, pl.ds(ROWS * w, ROWS), :]
        if op == 0:
            return dot_nn(tokens, w_in[:, pl.ds(start, TILE)])
        return dot_nt(tokens, w_out[pl.ds(start, TILE), :])

    def px_ref(w, op):
        return px.at[w % 2, op]

    def theirs(w, op):
        if w >= 2:
            wait_bytes(px_ref(w - 2, op), px_ss.at[w - 2, op])

        def tile(j, carry):
            at = pl.multiple_of(j * TILE, TILE)
            px[w % 2, op, :, pl.ds(at, TILE)] = product(
                w, op, pl.multiple_of((1 - c) * HALF + at, TILE)
            )
            return carry

        lax.fori_loop(0, HALF // TILE, tile, 0)
        remote(
            px_ref(w, op), pr.at[op, pl.ds(ROWS * w, ROWS)], px_ss.at[w, op], px_rs.at[w, op], mate
        ).start()

    def mine(w, op):
        def tile(j, carry):
            at = pl.multiple_of(j * TILE, TILE)
            pown[op, pl.ds(ROWS * w, ROWS), pl.ds(at, TILE)] = product(
                w, op, pl.multiple_of(c * HALF + at, TILE)
            )
            return carry

        lax.fori_loop(0, HALF // TILE, tile, 0)

    def wait_px(w, op):
        wait_bytes(pr.at[op, pl.ds(ROWS * w, ROWS)], px_rs.at[w, op])

    def own_term(w, op, k):
        at = pl.multiple_of(k * CH, CH)
        return pown[op, pl.ds(ROWS * w + at, CH), :] + pr[op, pl.ds(ROWS * w + at, CH), :]

    def slot(w, n):
        return pl.ds((7 * w + n) * CH, CH)

    def rs_send(w, op, n):
        k = z_chip(sign * (4 - n)) if n < 4 else z_chip(-sign * (7 - n))
        term = own_term(w, op, k)
        if n not in (0, 4):
            wait_bytes(rb.at[op, slot(w, n - 1)], rs_rs.at[w, op, n - 1])
            term = term + rb[op, slot(w, n - 1), :].astype(F32)
        sb[op, slot(w, n), :] = term.astype(BF)
        remote(
            sb.at[op, slot(w, n)], rb.at[op, slot(w, n)], rs_ss.at[w, op], rs_rs.at[w, op, n],
            fwd if n < 4 else back,
        ).start()

    def rs_final(w, op):
        total = own_term(w, op, z)
        for n in (6, 3):
            wait_bytes(rb.at[op, slot(w, n)], rs_rs.at[w, op, n])
            total = total + rb[op, slot(w, n), :].astype(F32)
        return total

    def chunk(w, k):
        return pl.ds(ROWS * w + pl.multiple_of(k * CH, CH), CH)

    def finish_hidden(w):
        hidden = rs_final(w, 0)
        act, slope = gelu_and_slope(hidden)
        ag[0, c, chunk(w, z), :] = act.astype(BF)
        ag[1, c, chunk(w, z), :] = (rs_final(w, 1) * slope).astype(BF)

    def ag_wait(w, op, n):
        wait_bytes(sb.at[op, slot(w, n)], ag_rs.at[w, op, n])

    def ag_send(w, op, n):
        k = z_chip(-sign * n) if n < 4 else z_chip(sign * (n - 4))
        if n not in (0, 4):
            ag_wait(w, op, n - 1)
        part = ag.at[op, c, chunk(w, k)]
        remote(part, part, ag_ss.at[w, op], ag_rs.at[w, op, n], fwd if n < 4 else back).start()

    def half_ref(w, op, half):
        return ag.at[op, half, pl.ds(ROWS * w, ROWS)]

    def x_send(w, op):
        ag_wait(w, op, 6)
        ag_wait(w, op, 3)
        remote(half_ref(w, op, c), half_ref(w, op, c), x_ss.at[w, op], x_rs.at[w, op], mate).start()

    def x_wait(w, op):
        wait_bytes(half_ref(w, op, 1 - c), x_rs.at[w, op])

    def outputs(w, op):
        tokens = pl.ds(ROWS * w, ROWS)

        def tile(j, carry):
            at = pl.ds(pl.multiple_of(j * TILE, TILE), TILE)
            if op == 0:
                total = dot_nn(ag[0, 0, tokens, :], w_out[pl.ds(0, HALF), at])
                total += dot_nn(ag[0, 1, tokens, :], w_out[pl.ds(HALF, HALF), at])
            else:
                total = dot_nt(ag[1, 0, tokens, :], w_in[at, pl.ds(0, HALF)])
                total += dot_nt(ag[1, 1, tokens, :], w_in[at, pl.ds(HALF, HALF)])
            ob[op, tokens, at] = total.astype(BF)
            return carry

        lax.fori_loop(0, HALF // TILE, tile, 0)
        push_outputs(w, op)

    def outputs_half(op, half, finish):
        w = WAVES - 1
        tokens = ag.at[op, half, pl.ds(ROWS * w, ROWS)]
        units = pl.ds(pl.multiple_of(half * HALF, HALF), HALF)

        def tile(j, carry):
            at = pl.ds(pl.multiple_of(j * TILE, TILE), TILE)
            if op == 0:
                total = dot_nn(tokens[...], w_out[units, at])
            else:
                total = dot_nt(tokens[...], w_in[at, units])
            if finish:
                ob[op, pl.ds(ROWS * w, ROWS), at] = (pown[op, pl.ds(0, ROWS), at] + total).astype(BF)
            else:
                pown[op, pl.ds(0, ROWS), at] = total
            return carry

        lax.fori_loop(0, HALF // TILE, tile, 0)
        if finish:
            push_outputs(w, op)

    def push_outputs(w, op):
        for n in (10, 6, 9, 14, 11, 5, 15, 7, 13, 8, 2, 4, 1, 12, 3):
            dy, dx = n // 4, n % 4
            remote(
                ob.at[op, pl.ds(ROWS * w + part_of(dy, dx), PART)],
                outr.at[op, n, pl.ds(PART * w, PART)],
                o_ss.at[w, op],
                o_rs.at[w, op],
                plane(dy, dx),
            ).start()

    def o_rows(w, op):
        return ob.at[op, pl.ds(ROWS * w + PART, ROWS - PART)]

    def weight_grad(which, hf):
        def tile(j, carry):
            units = pl.ds(pl.multiple_of(j * TILE, TILE), TILE)
            if which == 0:
                total = dot_tn(ag[0, hf, :, units], tg[1])
                gwo[pl.ds(pl.multiple_of(hf * HALF + j * TILE, TILE), TILE), :] = total.astype(BF)
            else:
                total = dot_tn(tg[0, :, units], ag[1, hf])
                gwi[units, pl.ds(pl.multiple_of(hf * HALF, HALF), HALF)] = total.astype(BF)
            return carry

        lax.fori_loop(0, 3, tile, 0)

    def tick(t):
        ages = [t - START[w] for w in range(WAVES)]
        for w in range(WAVES):
            age = ages[w]
            if 1 <= age <= 3:
                for op in range(2):
                    rs_send(w, op, age)
                    if age < 3:
                        rs_send(w, op, 4 + age)
            if age == 4:
                finish_hidden(w)
            if 4 <= age <= 7:
                for op in range(2):
                    ag_send(w, op, age - 4)
                    if age > 4:
                        ag_send(w, op, age - 1)
            if age == 8:
                x_send(w, 0)
                x_send(w, 1)
        for w in range(WAVES):
            if ages[w] == 0:
                for op in range(2):
                    wait_px(w, op)
                    rs_send(w, op, 0)
                    rs_send(w, op, 4)
        if t in (1, 2):
            forward(t + 1)
        for w in range(1, WAVES):
            if ages[w] == -1:
                for op in range(2):
                    wait_relay(w, op)
                    theirs(w, op)
                mine(w, 0)
                mine(w, 1)
        for w in range(WAVES - 1):
            if ages[w] == 8:
                for op in range(2):
                    x_wait(w, op)
                    outputs(w, op)

    push_cross(0, 0)
    push_cross(0, 1)
    forward(0)
    push_cross(1, 0)
    push_cross(1, 1)
    for load in loads:
        load.wait()
    for op in range(2):
        wait_relay(0, op)
        theirs(0, op)
    forward(1)
    for w in (2, 3):
        push_cross(w, 0)
        push_cross(w, 1)
    mine(0, 0)
    mine(0, 1)
    for t in range(START[-1] + 9):
        tick(t)
    last = WAVES - 1
    for op in range(2):
        outputs_half(op, c, False)
    for op in range(2):
        x_wait(last, op)
        outputs_half(op, 1 - c, True)
    weight_grad(0, c)
    weight_grad(0, 1 - c)
    weight_grad(1, c)
    weight_grad(1, 1 - c)

    def add_up(w, carry):
        mine_at = pl.multiple_of(w * ROWS, ROWS)
        at = pl.ds(pl.multiple_of(w * PART, PART), PART)
        for op, out in ((0, lo), (1, gt)):
            total = ob[op, pl.ds(mine_at, PART), :].astype(F32)
            for n in range(1, 16):
                total = total + outr[op, n, at, :].astype(F32)
            out[at, :] = total.astype(BF)
        return carry

    for w in range(last):
        for op in range(2):
            wait_bytes(o_rows(w, op), o_rs.at[w, op])
    lax.fori_loop(0, last, add_up, 0)
    for op in range(2):
        wait_bytes(o_rows(last, op), o_rs.at[last, op])
    lax.fori_loop(last, WAVES, add_up, 0)

    for w in range(WAVES):
        messages = pl.ds(7 * w * CH, 7 * CH)
        for op in range(2):
            wait_bytes(cross_rows(w, op), a_ss.at[op, w])
            wait_bytes(relay_rows(w, op), r_ss.at[op, w])
            if w >= WAVES - 2:
                wait_bytes(px_ref(w, op), px_ss.at[w, op])
            wait_bytes(sb.at[op, messages], rs_ss.at[w, op])
            wait_bytes(sb.at[op, messages], ag_ss.at[w, op])
            wait_bytes(half_ref(w, op, c), x_ss.at[w, op])
            wait_bytes(o_rows(w, op), o_ss.at[w, op])


OUT_SHAPES = ((64, HALF), (64, HALF), (HALF, 2 * HALF), (2 * HALF, HALF))


def write_out(*refs):
    sems = refs[8]
    copies = []
    for i, rows in ((2, 96), (3, 192), (0, 64), (1, 64)):
        for at in range(0, OUT_SHAPES[i][0], rows):
            part = pl.ds(at, rows)
            copies.append(pltpu.make_async_copy(refs[i].at[part], refs[4 + i].at[part], sems.at[len(copies)]))
    for copy in copies:
        copy.start()
    for copy in copies:
        copy.wait()


def body(tokens, w_in, w_out, grad_out):
    dma = pltpu.SemaphoreType.DMA
    any_spec = pl.BlockSpec(memory_space=pl.ANY)
    results = pl.pallas_call(
        kernel,
        name="ffn",
        out_shape=tuple(pltpu.VMEM(shape, BF) for shape in OUT_SHAPES),
        in_specs=[any_spec] * 4,
        out_specs=[pl.BlockSpec(memory_space=pltpu.VMEM)] * 4,
        scratch_shapes=[
            pltpu.VMEM((2, 64, HALF), BF),
            pltpu.VMEM((2, 1024, HALF), BF),
            pltpu.VMEM((HALF, 2 * HALF), BF),
            pltpu.VMEM((2 * HALF, HALF), BF),
            pltpu.VMEM((2, 1024, HALF), F32),
            pltpu.VMEM((2, 2, 256, HALF), F32),
            pltpu.VMEM((2, 1024, HALF), F32),
            pltpu.VMEM((2, 7 * 128, HALF), BF),
            pltpu.VMEM((2, 7 * 128, HALF), BF),
            pltpu.VMEM((2, 2, 1024, HALF), BF),
            pltpu.VMEM((2, 1024, HALF), BF),
            pltpu.VMEM((2, 16, 64, HALF), BF),
            dma((4,)),
            dma((2, WAVES)), dma((2, WAVES)),
            dma((2, WAVES)), dma((2, WAVES)),
            dma((WAVES, 2)), dma((WAVES, 2)),
            dma((WAVES, 2)), dma((WAVES, 2, 7)),
            dma((WAVES, 2)), dma((WAVES, 2, 7)),
            dma((WAVES, 2)), dma((WAVES, 2)),
            dma((WAVES, 2)), dma((WAVES, 2)),
        ],
        compiler_params=pltpu.CompilerParams(
            collective_id=0, has_side_effects=True, vmem_limit_bytes=50 << 20
        ),
        cost_estimate=pl.CostEstimate(flops=14500000000, bytes_accessed=10000000, transcendentals=2000000),
    )(tokens, w_in, w_out, grad_out)
    return pl.pallas_call(
        write_out,
        name="write_out",
        out_shape=tuple(jax.ShapeDtypeStruct(shape, BF) for shape in OUT_SHAPES),
        in_specs=[any_spec] * 4,
        out_specs=[any_spec] * 4,
        compiler_params=pltpu.CompilerParams(vmem_limit_bytes=1 << 20),
        scratch_shapes=[dma((18,))],
        cost_estimate=pl.CostEstimate(flops=0, bytes_accessed=10000000, transcendentals=0),
    )(*[pltpu.with_memory_space_constraint(r, pltpu.VMEM) for r in results])


def solution(mesh):
    placed = (P("col", "row"), P("row", "col"), P("col", "row"), P("col", "row"))
    return jax.shard_map(
        body,
        mesh=mesh,
        in_specs=placed,
        out_specs=(P("col", "row"), P("col", "row"), P("row", "col"), P("col", "row")),
        check_vma=False,
    )
```

```python
import jax
import jax.numpy as jnp
from jax import lax
from jax.experimental import pallas as pl
from jax.experimental.pallas import tpu as pltpu
from jax.sharding import PartitionSpec as P

MESH = pl.DeviceIdType.MESH
BF = jnp.bfloat16
F32 = jnp.float32
gelu_coef = 0.7978845608

WAVES = 4
ROWS = 256
PART = 16
START = [0, 2, 4, 6]
CH = 32
HALF = 768
TILE = 256


def part_of(dy, dx):
    if dy == 0:
        return PART * dx
    if dx == 0:
        return PART * (3 + dy)
    return PART * (7 + 3 * (dy - 1) + dx - 1)


def gelu_and_slope(h):
    t = jnp.tanh(gelu_coef * (h + 0.044715 * h * h * h))
    act = 0.5 * h * (1.0 + t)
    slope = 0.5 * (1.0 + t) + 0.5 * h * (1.0 - t * t) * gelu_coef * (1.0 + 3.0 * 0.044715 * h * h)
    return act, slope


def dot_nn(a, b):
    return lax.dot_general(a, b, (((1,), (0,)), ((), ())), preferred_element_type=F32)


def dot_nt(a, b):
    return lax.dot_general(a, b, (((1,), (1,)), ((), ())), preferred_element_type=F32)


def dot_tn(a, b):
    return lax.dot_general(a, b, (((0,), (0,)), ((), ())), preferred_element_type=F32)


def kernel(
    tok_hbm, win_hbm, wout_hbm, gout_hbm,
    lo, gt, gwi, gwo,
    shard, tg, w_in, w_out, pown, px, pr, sb, rb, ag, ob, outr,
    loc_sem, a_ss, a_rs, r_ss, r_rs, px_ss, px_rs, rs_ss, rs_rs, ag_ss, ag_rs, x_ss, x_rs, o_ss, o_rs,
):
    row, col = lax.axis_index("row"), lax.axis_index("col")
    z, c = row // 2, row % 2
    y, x = col // 4, col % 4
    sign = 1 - 2 * c

    def z_chip(d):
        return (z + d + 16) % 8

    fwd = (z_chip(sign) * 2 + c, col)
    back = (z_chip(-sign) * 2 + c, col)
    mate = (z * 2 + 1 - c, col)

    def plane(dy, dx):
        return (row, ((y + dy + 4) % 4) * 4 + (x + dx + 4) % 4)

    shards = [
        pltpu.make_async_copy(tok_hbm, shard.at[0], loc_sem.at[0]),
        pltpu.make_async_copy(gout_hbm, shard.at[1], loc_sem.at[1]),
    ]
    loads = [
        pltpu.make_async_copy(win_hbm, w_in, loc_sem.at[2]),
        pltpu.make_async_copy(wout_hbm, w_out, loc_sem.at[3]),
    ]
    for load in shards + loads:
        load.start()

    barrier = pltpu.get_barrier_semaphore()
    greet = [fwd, back, mate] + [plane(d // 4, d % 4) for d in range(1, 16)]
    for dev in greet:
        pl.semaphore_signal(barrier, inc=1, device_id=dev, device_id_type=MESH)
    for load in shards:
        load.wait()
    for arr in range(2):
        for w in range(WAVES):
            tg[arr, pl.ds(ROWS * w, PART), :] = shard[arr, pl.ds(PART * w, PART), :]
    pl.semaphore_wait(barrier, len(greet))

    def remote(src, dst, ss, rs, dev):
        return pltpu.make_async_remote_copy(
            src_ref=src, dst_ref=dst, send_sem=ss, recv_sem=rs, device_id=dev, device_id_type=MESH
        )

    def wait_bytes(ref, sem):
        pltpu.make_async_copy(ref, ref, sem).wait()

    def push_cross(w, arr):
        for dy, dx in ((0, 2), (2, 0), (0, 1), (1, 0), (0, 3), (3, 0)):
            remote(
                shard.at[arr, pl.ds(PART * w, PART)],
                tg.at[arr, pl.ds(ROWS * w + part_of(dy, dx), PART)],
                a_ss.at[0],
                a_rs.at[arr, w],
                plane(-dy, -dx),
            ).start()

    def cross_rows(w, arr):
        return tg.at[arr, pl.ds(ROWS * w + PART, 6 * PART)]

    def wait_cross(w, arr):
        wait_bytes(cross_rows(w, arr), a_rs.at[arr, w])

    def push_relay(w, arr):
        def send(src, dst, rows, dev):
            remote(
                tg.at[arr, pl.ds(ROWS * w + src, rows)],
                tg.at[arr, pl.ds(ROWS * w + dst, rows)],
                r_ss.at[0],
                r_rs.at[arr, w],
                dev,
            ).start()

        for d in (1, 3):
            send(part_of(0, 1), part_of(d, 1), 3 * PART, plane(-d, 0))
            send(part_of(2, 0), part_of(2, d), PART, plane(0, -d))
        send(part_of(2, 0), part_of(2, 2), PART, plane(0, -2))

    def relay_rows(w, arr):
        return tg.at[arr, pl.ds(ROWS * w + 7 * PART, 9 * PART)]

    def wait_relay(w, arr):
        wait_bytes(relay_rows(w, arr), r_rs.at[arr, w])

    def forward(w):
        for arr in range(2):
            wait_cross(w, arr)
            push_relay(w, arr)

    def product(w, op, start):
        tokens = tg[op, pl.ds(ROWS * w, ROWS), :]
        if op == 0:
            return dot_nn(tokens, w_in[:, pl.ds(start, TILE)])
        return dot_nt(tokens, w_out[pl.ds(start, TILE), :])

    def px_ref(w, op):
        return px.at[w % 2, op]

    def theirs(w, op):
        if w >= 2:
            wait_bytes(px_ref(w - 2, op), px_ss.at[w - 2, op])

        def tile(j, carry):
            at = pl.multiple_of(j * TILE, TILE)
            px[w % 2, op, :, pl.ds(at, TILE)] = product(
                w, op, pl.multiple_of((1 - c) * HALF + at, TILE)
            )
            return carry

        lax.fori_loop(0, HALF // TILE, tile, 0)
        remote(
            px_ref(w, op), pr.at[op, pl.ds(ROWS * w, ROWS)], px_ss.at[w, op], px_rs.at[w, op], mate
        ).start()

    def mine(w, op):
        def tile(j, carry):
            at = pl.multiple_of(j * TILE, TILE)
            pown[op, pl.ds(ROWS * w, ROWS), pl.ds(at, TILE)] = product(
                w, op, pl.multiple_of(c * HALF + at, TILE)
            )
            return carry

        lax.fori_loop(0, HALF // TILE, tile, 0)

    def wait_px(w, op):
        wait_bytes(pr.at[op, pl.ds(ROWS * w, ROWS)], px_rs.at[w, op])

    def own_term(w, op, k):
        at = pl.multiple_of(k * CH, CH)
        return pown[op, pl.ds(ROWS * w + at, CH), :] + pr[op, pl.ds(ROWS * w + at, CH), :]

    def slot(w, n):
        return pl.ds((7 * w + n) * CH, CH)

    def rs_send(w, op, n):
        way = sign if op == 0 else -sign
        k = z_chip(way * (4 - n)) if n < 4 else z_chip(-way * (7 - n))
        term = own_term(w, op, k)
        if n not in (0, 4):
            wait_bytes(rb.at[op, slot(w, n - 1)], rs_rs.at[w, op, n - 1])
            term = term + rb[op, slot(w, n - 1), :].astype(F32)
        sb[op, slot(w, n), :] = term.astype(BF)
        remote(
            sb.at[op, slot(w, n)], rb.at[op, slot(w, n)], rs_ss.at[0], rs_rs.at[w, op, n],
            fwd if (n < 4) == (op == 0) else back,
        ).start()

    def rs_final(w, op):
        total = own_term(w, op, z)
        for n in (6, 3):
            wait_bytes(rb.at[op, slot(w, n)], rs_rs.at[w, op, n])
            total = total + rb[op, slot(w, n), :].astype(F32)
        return total

    def chunk(w, k):
        return pl.ds(ROWS * w + pl.multiple_of(k * CH, CH), CH)

    def finish_hidden(w):
        hidden = rs_final(w, 0)
        act, slope = gelu_and_slope(hidden)
        ag[0, c, chunk(w, z), :] = act.astype(BF)
        ag[1, c, chunk(w, z), :] = (rs_final(w, 1) * slope).astype(BF)

    def ag_wait(w, op, n):
        wait_bytes(sb.at[op, slot(w, n)], ag_rs.at[w, op, n])

    def ag_send(w, op, n):
        way = sign if op == 0 else -sign
        k = z_chip(-way * n) if n < 4 else z_chip(way * (n - 4))
        if n not in (0, 4):
            ag_wait(w, op, n - 1)
        part = ag.at[op, c, chunk(w, k)]
        remote(part, part, ag_ss.at[0], ag_rs.at[w, op, n], fwd if (n < 4) == (op == 0) else back).start()

    def half_ref(w, op, half):
        return ag.at[op, half, pl.ds(ROWS * w, ROWS)]

    def x_send(w, op):
        ag_wait(w, op, 6)
        ag_wait(w, op, 3)
        remote(half_ref(w, op, c), half_ref(w, op, c), x_ss.at[0], x_rs.at[w, op], mate).start()

    def x_wait(w, op):
        wait_bytes(half_ref(w, op, 1 - c), x_rs.at[w, op])

    def outputs(w, op):
        tokens = pl.ds(ROWS * w, ROWS)

        def tile(j, carry):
            at = pl.ds(pl.multiple_of(j * TILE, TILE), TILE)
            if op == 0:
                total = dot_nn(ag[0, 0, tokens, :], w_out[pl.ds(0, HALF), at])
                total += dot_nn(ag[0, 1, tokens, :], w_out[pl.ds(HALF, HALF), at])
            else:
                total = dot_nt(ag[1, 0, tokens, :], w_in[at, pl.ds(0, HALF)])
                total += dot_nt(ag[1, 1, tokens, :], w_in[at, pl.ds(HALF, HALF)])
            ob[op, tokens, at] = total.astype(BF)
            return carry

        lax.fori_loop(0, HALF // TILE, tile, 0)
        push_outputs(w, op)

    def outputs_half(op, half, finish):
        w = WAVES - 1
        tokens = ag.at[op, half, pl.ds(ROWS * w, ROWS)]
        units = pl.ds(pl.multiple_of(half * HALF, HALF), HALF)

        def tile(j, carry):
            at = pl.ds(pl.multiple_of(j * TILE, TILE), TILE)
            if op == 0:
                total = dot_nn(tokens[...], w_out[units, at])
            else:
                total = dot_nt(tokens[...], w_in[at, units])
            if finish:
                ob[op, pl.ds(ROWS * w, ROWS), at] = (pown[op, pl.ds(0, ROWS), at] + total).astype(BF)
            else:
                pown[op, pl.ds(0, ROWS), at] = total
            return carry

        lax.fori_loop(0, HALF // TILE, tile, 0)
        if finish:
            push_outputs(w, op)

    def push_outputs(w, op):
        for n in (10, 6, 9, 14, 11, 5, 15, 7, 13, 8, 2, 4, 1, 12, 3):
            dy, dx = n // 4, n % 4
            remote(
                ob.at[op, pl.ds(ROWS * w + part_of(dy, dx), PART)],
                outr.at[op, n, pl.ds(PART * w, PART)],
                o_ss.at[0],
                o_rs.at[w, op],
                plane(dy, dx),
            ).start()

    def o_rows(w, op):
        return ob.at[op, pl.ds(ROWS * w + PART, ROWS - PART)]

    def weight_grad(which, hf):
        def tile(j, carry):
            units = pl.ds(pl.multiple_of(j * TILE, TILE), TILE)
            if which == 0:
                total = dot_tn(ag[0, hf, :, units], tg[1])
                gwo[pl.ds(pl.multiple_of(hf * HALF + j * TILE, TILE), TILE), :] = total.astype(BF)
            else:
                total = dot_tn(tg[0, :, units], ag[1, hf])
                gwi[units, pl.ds(pl.multiple_of(hf * HALF, HALF), HALF)] = total.astype(BF)
            return carry

        lax.fori_loop(0, 3, tile, 0)

    def tick(t):
        ages = [t - START[w] for w in range(WAVES)]
        for w in range(WAVES):
            age = ages[w]
            if 1 <= age <= 3:
                for op in range(2):
                    rs_send(w, op, age)
                    if age < 3:
                        rs_send(w, op, 4 + age)
            if age == 4:
                finish_hidden(w)
            if 4 <= age <= 7:
                for op in range(2):
                    ag_send(w, op, age - 4)
                    if age > 4:
                        ag_send(w, op, age - 1)
            if age == 8:
                x_send(w, 0)
                x_send(w, 1)
        for w in range(WAVES):
            if ages[w] == 0:
                for op in range(2):
                    wait_px(w, op)
                    rs_send(w, op, 0)
                    rs_send(w, op, 4)
        if t in (1, 2):
            forward(t + 1)
        for w in range(1, WAVES):
            if ages[w] == -1:
                for op in range(2):
                    wait_relay(w, op)
                    theirs(w, op)
                mine(w, 0)
                mine(w, 1)
        for w in range(WAVES - 1):
            if ages[w] == 8:
                for op in range(2):
                    x_wait(w, op)
                    outputs(w, op)

    push_cross(0, 0)
    push_cross(0, 1)
    forward(0)
    push_cross(1, 0)
    push_cross(1, 1)
    for load in loads:
        load.wait()
    for op in range(2):
        wait_relay(0, op)
        theirs(0, op)
    forward(1)
    for w in (2, 3):
        push_cross(w, 0)
        push_cross(w, 1)
    mine(0, 0)
    mine(0, 1)
    for t in range(START[-1] + 9):
        tick(t)
    last = WAVES - 1
    for op in range(2):
        outputs_half(op, c, False)
    for op in range(2):
        x_wait(last, op)
        outputs_half(op, 1 - c, True)
    weight_grad(0, c)
    weight_grad(0, 1 - c)
    weight_grad(1, c)
    weight_grad(1, 1 - c)

    def add_up(w, carry):
        mine_at = pl.multiple_of(w * ROWS, ROWS)
        at = pl.ds(pl.multiple_of(w * PART, PART), PART)
        for op, out in ((0, lo), (1, gt)):
            total = ob[op, pl.ds(mine_at, PART), :].astype(F32)
            for n in range(1, 16):
                total = total + outr[op, n, at, :].astype(F32)
            out[at, :] = total.astype(BF)
        return carry

    for w in range(last):
        for op in range(2):
            wait_bytes(o_rows(w, op), o_rs.at[w, op])
    lax.fori_loop(0, last, add_up, 0)
    for op in range(2):
        wait_bytes(o_rows(last, op), o_rs.at[last, op])
    lax.fori_loop(last, WAVES, add_up, 0)

    wait_bytes(tg.at[0, pl.ds(0, 8 * 6 * PART)], a_ss.at[0])
    wait_bytes(tg.at[:, pl.ds(0, 4 * 9 * PART)], r_ss.at[0])
    wait_bytes(sb, rs_ss.at[0])
    wait_bytes(sb, ag_ss.at[0])
    wait_bytes(tg, x_ss.at[0])
    wait_bytes(ob.at[:, pl.ds(0, 4 * 15 * PART)], o_ss.at[0])
    for w in (WAVES - 2, WAVES - 1):
        for op in range(2):
            wait_bytes(px_ref(w, op), px_ss.at[w, op])


OUT_SHAPES = ((64, HALF), (64, HALF), (HALF, 2 * HALF), (2 * HALF, HALF))


def write_out(*refs):
    sems = refs[8]
    copies = []
    for i, rows in ((2, 96), (3, 192), (0, 64), (1, 64)):
        for at in range(0, OUT_SHAPES[i][0], rows):
            part = pl.ds(at, rows)
            copies.append(pltpu.make_async_copy(refs[i].at[part], refs[4 + i].at[part], sems.at[i]))
    for copy in copies:
        copy.start()
    for i in range(4):
        pltpu.make_async_copy(refs[i], refs[4 + i], sems.at[i]).wait()


def body(tokens, w_in, w_out, grad_out):
    dma = pltpu.SemaphoreType.DMA
    any_spec = pl.BlockSpec(memory_space=pl.ANY)
    results = pl.pallas_call(
        kernel,
        name="ffn",
        out_shape=tuple(pltpu.VMEM(shape, BF) for shape in OUT_SHAPES),
        in_specs=[any_spec] * 4,
        out_specs=[pl.BlockSpec(memory_space=pltpu.VMEM)] * 4,
        scratch_shapes=[
            pltpu.VMEM((2, 64, HALF), BF),
            pltpu.VMEM((2, 1024, HALF), BF),
            pltpu.VMEM((HALF, 2 * HALF), BF),
            pltpu.VMEM((2 * HALF, HALF), BF),
            pltpu.VMEM((2, 1024, HALF), F32),
            pltpu.VMEM((2, 2, 256, HALF), F32),
            pltpu.VMEM((2, 1024, HALF), F32),
            pltpu.VMEM((2, 7 * 128, HALF), BF),
            pltpu.VMEM((2, 7 * 128, HALF), BF),
            pltpu.VMEM((2, 2, 1024, HALF), BF),
            pltpu.VMEM((2, 1024, HALF), BF),
            pltpu.VMEM((2, 16, 64, HALF), BF),
            dma((4,)),
            dma((1,)), dma((2, WAVES)),
            dma((1,)), dma((2, WAVES)),
            dma((WAVES, 2)), dma((WAVES, 2)),
            dma((1,)), dma((WAVES, 2, 7)),
            dma((1,)), dma((WAVES, 2, 7)),
            dma((1,)), dma((WAVES, 2)),
            dma((1,)), dma((WAVES, 2)),
        ],
        compiler_params=pltpu.CompilerParams(
            collective_id=0, has_side_effects=True, vmem_limit_bytes=50 << 20
        ),
        cost_estimate=pl.CostEstimate(flops=14500000000, bytes_accessed=10000000, transcendentals=2000000),
    )(tokens, w_in, w_out, grad_out)
    return pl.pallas_call(
        write_out,
        name="write_out",
        out_shape=tuple(jax.ShapeDtypeStruct(shape, BF) for shape in OUT_SHAPES),
        in_specs=[any_spec] * 4,
        out_specs=[any_spec] * 4,
        compiler_params=pltpu.CompilerParams(vmem_limit_bytes=1 << 20),
        scratch_shapes=[dma((4,))],
        cost_estimate=pl.CostEstimate(flops=0, bytes_accessed=10000000, transcendentals=0),
    )(*[pltpu.with_memory_space_constraint(r, pltpu.VMEM) for r in results])


def solution(mesh):
    placed = (P("col", "row"), P("row", "col"), P("col", "row"), P("col", "row"))
    return jax.shard_map(
        body,
        mesh=mesh,
        in_specs=placed,
        out_specs=(P("col", "row"), P("col", "row"), P("row", "col"), P("col", "row")),
        check_vma=False,
    )
```
